32 devices in a mesh: frag: 2 (over y), space: 4 (over z), aux: 2 (over x), sub: 2 (over core).
Axes of the slice: x: 2, y: 2, z: 4, core: 2. Of those that a mesh axis runs over, the one named last changes fastest.
Arguments:
- densities: bfloat16 [128, 128, 256], P(('frag', 'space', 'sub')), parts along dimension 0, may hold values from -6 to 6
- three_centre: bfloat16 [128, 24, 128, 128], P(('frag', 'space', 'sub'), 'aux'), parts along dimension 0, may hold values from -0.0625 to 0.0625
- block_tile: int32 [128, 24], P(('frag', 'space', 'sub'), 'aux'), parts along dimension 0, may hold values from 0 to 31
- owner_domain: int32 [16, 2, 32, 1], P(('frag', 'space', 'sub'), 'aux'), parts along dimension 0, may hold values from 0 to 3; in each aligned block of 32 rows (0 to 31, 32 to 63, ..., all dimensions but the last counted through in order) at most 16 rows name the same one
- owner_tile: int32 [16, 2, 32], P(('frag', 'space', 'sub'), 'aux'), parts along dimension 0, may hold values from 0 to 2
- metric_inverse: bfloat16 [48, 8, 128, 128], P(('frag', 'space', 'aux'), 'sub'), parts along dimension 0, may hold values from -0.1875 to 0.1875
- metric_columns: int32 [48, 8], P(('frag', 'space', 'aux'), 'sub'), parts along dimension 0, may hold values from 0 to 17
Outputs:
- coulomb: bfloat16 [128, 128, 256], P(('frag', 'space', 'sub'), 'aux'), parts along dimension 0
The draws below stay inside these ranges and needn't reach their ends.
There are 2 independent parts, one for each index of `frag`. The reference program is written for one: setup_inputs(seed, part) draws one part's arguments, and reference() takes and returns one part's arrays. A program takes and returns all parts, laid end to end along the dimension named above; each array names one. Nothing has to cross between parts.
Inputs may be any that keep to these rules, and one draw needn't show every extreme that they name: `block_tile`: index into the 32 touched tiles of the device holding the block. `owner_domain`: among the 32 touched tiles of one device at most 16 name the same domain; some device has exactly 16.
All inputs are finite; a program needn't handle non-finite values.
Results may differ from the reference program's by a relative error of at most 0.019.
Values may be sent and summed in bfloat16 or wider, within the bound.
No kernel may reach another device: no remote copies, remote signals or barrier semaphores. Data moves between devices by JAX's collectives and lax.ppermute only.
A program may use at most 64 MiB of HBM per device.

```python
import math
import jax
import jax.numpy as jnp
import numpy as np
from jax import lax

TW = 128
NDEN = 256
PB_DEV = 8
K_DEV = 12
NT_DEV = 32
AT_DEV = 3
MB = 8
CAP = 16
NPB = 64
KT = 24
NAT = 24
WIN = 18
N_SPACE = 4
N_AUX = 2
N_SUB = 2


def plant(entries, rng, least, top_value):
    longest = entries.shape.index(max(entries.shape))
    spots = []
    for shift in (0, 1):
        where = [jax.random.randint(jax.random.fold_in(rng, axis), (), 0, length) for axis, length in enumerate(entries.shape)]
        where[longest] = (where[longest] + shift) % entries.shape[longest]
        spots.append(tuple(where))
    return entries.at[spots[0]].set(least).at[spots[1]].set(top_value)


def level_of(own_key, extent, shards, smallest, high):
    loudness = 1.0
    for dim, parts in shards:
        draws = jax.random.uniform(jax.random.fold_in(jax.random.fold_in(own_key, 6), dim), (parts,), jnp.float32, smallest / len(shards), high / len(shards))
        loudness = loudness * jnp.repeat(jnp.exp(draws), extent[dim] // parts).reshape((-1,) + (1,) * (len(extent) - 1 - dim))
    return loudness


def assign_block(stream_key, own, number, rows, number_of, top, reach, skew):
    order = jax.random.permutation(stream_key, number_of)
    packed, usual = portions_of(number_of, rows * top, reach, skew, True), portions_of(number_of, rows * top, reach, skew, False)
    places = jnp.arange(number_of)

    def named(sizes, turn):
        used = int((sizes > 0).sum())
        fixed = max(1, used // 4)
        moved = fixed + (places - fixed + turn * (used - fixed)) % max(1, number_of - fixed)
        return jnp.zeros((number_of,), jnp.int32).at[order[jnp.where(places < fixed, places, moved)]].set(jnp.asarray(sizes, jnp.int32))

    sizes = jnp.where(number % 4 == 0, named(packed, number // 4), named(usual, number - number // 4 - 1))
    mixed = jax.random.permutation(jax.random.fold_in(own, 3), number_of)
    source_of, taker = mixed[0:number_of // 2 * 2:2], mixed[1:number_of // 2 * 2:2]
    room = jnp.minimum(sizes[source_of] - 1, reach - sizes[taker]) // 2
    room = jnp.where((source_of == order[0]) | (taker == order[0]) | (sizes[taker] == 0), 0, jnp.maximum(room, 0))
    moved = jax.random.randint(jax.random.fold_in(own, 4), (number_of // 2,), 0, 1 << 20) % (room + 1)
    sizes = sizes.at[source_of].add(-moved).at[taker].add(moved)
    labels = jnp.searchsorted(jnp.cumsum(sizes), jnp.arange(rows * top), side="right").astype(jnp.int32)
    table = labels.reshape(top, rows).T
    table = table[jax.random.permutation(jax.random.fold_in(own, 1), rows)]
    turn = jax.random.randint(jax.random.fold_in(own, 2), (rows, 1), 0, top)
    return jnp.take_along_axis(table, (jnp.arange(top)[None, :] + turn) % top, axis=1)


def portions_of(number_of, total, bound, lean, full):
    loads = [(1 << 20) // math.isqrt(grade ** lean) + 1 for grade in range(1, number_of + 1)]
    largest = bound if full else min(bound, max(-(-total // number_of), total * loads[0] // sum(loads)))
    least = 1 if total - largest >= number_of - 1 else 0
    holding, surplus = [largest] + [least] * (number_of - 1), total - largest - least * (number_of - 1)
    while surplus > 0:
        candidates = [i for i in range(1, number_of) if holding[i] < largest] or [i for i in range(1, number_of) if holding[i] < bound]
        pool, left = sum([loads[i] for i in candidates]), surplus
        for i in candidates:
            more = min(bound - holding[i], max(1, left * loads[i] // pool), surplus)
            holding[i] = holding[i] + more
            surplus = surplus - more
    return np.array(holding)


def normal_values(stream_key, dims, scale, limit, cuts=(), kind=jnp.bfloat16):
    entries = jax.random.normal(stream_key, dims, jnp.float32) * scale
    if len(cuts) > 0:
        entries = level_of(stream_key, dims, cuts, -0.22, 0.18) * entries
    return jnp.clip(entries, min=-limit, max=limit).astype(kind)


def setup_inputs(seed: int = 0, part: int = 0) -> dict:
    keys = jax.random.split(jax.random.key(seed), 8)
    part_splits = jax.random.split(jax.random.fold_in(keys[7], part), 8)
    densities = normal_values(part_splits[0], (NPB, TW, NDEN), 1.0, 6.0, ((0, 8),))
    three_centre = normal_values(part_splits[1], (NPB, KT, TW, TW), (TW * PB_DEV * K_DEV * N_SUB // AT_DEV) ** -0.5, 0.0625, ((0, 8), (1, 2)))
    block_tile = plant(jax.random.randint(part_splits[2], (NPB, KT), 0, NT_DEV), jax.random.fold_in(part_splits[2], 1), 0, NT_DEV - 1).astype(jnp.int32)
    owner_domain_keys = jax.random.split(jax.random.fold_in(part_splits[3], 1), (N_SPACE * N_SUB) * N_AUX * NT_DEV // NT_DEV)
    owner_domain_turns = jax.random.permutation(jax.random.fold_in(part_splits[3], 3), (N_SPACE * N_SUB) * N_AUX * NT_DEV // NT_DEV)
    owner_domain = jax.vmap(lambda own, number: assign_block(jax.random.fold_in(part_splits[3], 2), own, number, NT_DEV, N_SPACE, 1, CAP, 2))(owner_domain_keys, owner_domain_turns).reshape((N_SPACE * N_SUB, N_AUX, NT_DEV, 1))
    owner_tile = plant(jax.random.randint(part_splits[4], (N_SPACE * N_SUB, N_AUX, NT_DEV), 0, AT_DEV), jax.random.fold_in(part_splits[4], 1), 0, AT_DEV - 1).astype(jnp.int32)
    metric_inverse = normal_values(part_splits[5], (NAT, MB, TW, TW), (TW * MB) ** -0.5, 0.1875, ((0, 8), (1, 2)))
    metric_columns = plant(jax.random.randint(part_splits[6], (NAT, MB), 0, WIN), jax.random.fold_in(part_splits[6], 1), 0, WIN - 1).astype(jnp.int32)
    return dict(densities=densities, three_centre=three_centre, block_tile=block_tile, owner_domain=owner_domain, owner_tile=owner_tile, metric_inverse=metric_inverse, metric_columns=metric_columns)


def reference(densities, three_centre, block_tile, owner_domain, owner_tile, metric_inverse, metric_columns):
    groups = N_SPACE * N_SUB
    blocks = three_centre.reshape(groups, PB_DEV, N_AUX, K_DEV, TW, TW)
    density_rows = densities.reshape(groups, PB_DEV, TW, NDEN)
    block_index = block_tile.reshape(groups, PB_DEV, N_AUX, K_DEV)
    aux_column = jnp.arange(N_AUX, dtype=jnp.int32)
    slot_table = (owner_domain.reshape(groups, N_AUX, NT_DEV) * N_AUX + aux_column[None, :, None]) * AT_DEV + owner_tile.reshape(groups, N_AUX, NT_DEV)
    touched_range = jnp.arange(NT_DEV, dtype=jnp.int32)

    def add_group(totals, group_index):
        contrib = jnp.einsum("pakrc,prn->pakcn", blocks[group_index].astype(jnp.float32), density_rows[group_index].astype(jnp.float32))
        chooser = (block_index[group_index][..., None] == touched_range).astype(jnp.float32)
        partial_sum = lax.optimization_barrier(jnp.einsum("pakt,pakcn->atcn", chooser, contrib).astype(jnp.bfloat16))
        totals = totals.at[slot_table[group_index].reshape(-1)].add(partial_sum.astype(jnp.float32).reshape(-1, TW, NDEN))
        return totals, None

    zero_start = jnp.zeros((NAT, TW, NDEN), jnp.float32)
    fitted, _ = lax.scan(add_group, zero_start, jnp.arange(groups, dtype=jnp.int32))
    fitted_low = lax.optimization_barrier(fitted.astype(jnp.bfloat16)).astype(jnp.float32)
    domain_tiles = fitted_low.reshape(N_SPACE, N_AUX * AT_DEV, TW, NDEN)
    padded = jnp.pad(domain_tiles, ((1, 1), (0, 0), (0, 0), (0, 0)))
    metric_rows = metric_inverse.reshape(N_SPACE, N_AUX * AT_DEV, MB, TW, TW)
    column_rows = metric_columns.reshape(N_SPACE, N_AUX * AT_DEV, MB)

    def solve_domain(domain_index):
        window = lax.dynamic_slice_in_dim(padded, domain_index, 3, 0).reshape(WIN, TW, NDEN)
        chosen = window[column_rows[domain_index]]
        return jnp.einsum("qjcr,qjrn->qcn", metric_rows[domain_index].astype(jnp.float32), chosen).astype(jnp.bfloat16)

    coefficients = lax.map(solve_domain, jnp.arange(N_SPACE, dtype=jnp.int32)).reshape(NAT, TW, NDEN)

    def build_group(group_index):
        needed = coefficients[slot_table[group_index]]
        picked = needed[aux_column[None, :, None], block_index[group_index]]
        return jnp.einsum("pakrc,pakcn->prn", blocks[group_index].astype(jnp.float32), picked.astype(jnp.float32)).astype(jnp.bfloat16)

    coulomb = lax.map(build_group, jnp.arange(groups, dtype=jnp.int32))
    return coulomb.reshape(groups * PB_DEV, TW, NDEN)
```

```python
import functools

import jax
import jax.numpy as jnp
from jax import lax
from jax.experimental import pallas as pl
from jax.experimental.pallas import tpu as pltpu
from jax.sharding import PartitionSpec as P

BF16 = jnp.bfloat16
F32 = jnp.float32
NT = (((1,), (1,)), ((), ()))
VMEM_LIMIT = 48 * 1024 * 1024


def fit_kernel(owned, half, tile_ref, domain_ref, number_ref, d_ref, t_ref, keep_ref, send_ref, acc):
    step = pl.program_id(0)
    me = lax.axis_index("space")
    mine = lax.axis_index("sub")
    listed = t_ref.shape[1]

    @pl.when(step == 0)
    def _():
        acc[...] = jnp.zeros_like(acc)

    rows = jnp.transpose(d_ref[0])
    for k in range(listed):
        touched = tile_ref[step, k]
        slot = jnp.bitwise_xor(domain_ref[touched], me) * owned + number_ref[touched]
        acc[slot] += jnp.dot(rows, t_ref[0, k], preferred_element_type=F32)

    @pl.when(step == pl.num_programs(0) - 1)
    def _():
        keep_ref[...] = acc[:, pl.ds(pl.multiple_of(mine * half, half), half), :].astype(BF16)
        send_ref[...] = acc[:, pl.ds(pl.multiple_of((1 - mine) * half, half), half), :].astype(BF16)


def fit(block_tile, domain, number, densities, three_centre, domains, owned):
    blocks, listed, width, _ = three_centre.shape
    columns = densities.shape[2]
    half = columns // 2
    slots = domains * owned
    out = jax.ShapeDtypeStruct((slots, half, width), BF16)
    return pl.pallas_call(
        functools.partial(fit_kernel, owned, half),
        grid_spec=pltpu.PrefetchScalarGridSpec(
            num_scalar_prefetch=3,
            grid=(blocks,),
            in_specs=[
                pl.BlockSpec((1, width, columns), lambda p, *_: (p, 0, 0)),
                pl.BlockSpec((1, listed, width, width), lambda p, *_: (p, 0, 0, 0)),
            ],
            out_specs=[pl.BlockSpec((slots, half, width), lambda p, *_: (0, 0, 0))] * 2,
            scratch_shapes=[pltpu.VMEM((slots, columns, width), F32)],
        ),
        out_shape=[out, out],
        compiler_params=pltpu.CompilerParams(vmem_limit_bytes=VMEM_LIMIT),
        cost_estimate=pl.CostEstimate(
            flops=2 * blocks * listed * width * width * columns,
            bytes_accessed=2 * (three_centre.size + densities.size),
            transcendentals=0,
        ),
        name="fit",
    )(block_tile, domain, number, densities, three_centre)


def metric_kernel(owned, count, mine_cols, peer_cols, near_ref, even_ref, odd_ref, m_ref, pm_ref, out_ref, window):
    me = lax.axis_index("space")
    aux = lax.axis_index("aux")
    own = owned * count
    window[:own] = near_ref[...]
    window[own : 2 * own] = even_ref[...]
    window[2 * own :] = odd_ref[...]

    def place(column):
        zone = column // own
        rest = column % own
        side = jnp.where((zone == 2) == (me % 2 == 0), 1, 2)
        block = jnp.where(zone == 1, 0, side)
        turned = (rest // owned + count - aux) % count
        return block * own + turned * owned + rest % owned

    for q in range(m_ref.shape[0]):
        picked, blocks = [], []
        for cols, mat in ((mine_cols, m_ref), (peer_cols, pm_ref)):
            for m in range(mat.shape[1]):
                picked.append(window[place(cols[q, m])])
                blocks.append(mat[q, m])
        out_ref[q] = lax.dot_general(
            jnp.concatenate(picked, axis=1),
            jnp.concatenate(blocks, axis=1),
            NT,
            preferred_element_type=F32,
        ).astype(BF16)


def metric(mine_cols, peer_cols, near, even, odd, m, pm, count):
    owned, listed, width, _ = m.shape
    half = near.shape[1]
    return pl.pallas_call(
        functools.partial(metric_kernel, owned, count),
        in_specs=[pl.BlockSpec(memory_space=pltpu.SMEM)] * 2 + [pl.BlockSpec(memory_space=pltpu.VMEM)] * 5,
        out_specs=pl.BlockSpec(memory_space=pltpu.VMEM),
        out_shape=jax.ShapeDtypeStruct((owned, half, width), BF16),
        scratch_shapes=[pltpu.VMEM((3 * owned * count, half, width), BF16)],
        compiler_params=pltpu.CompilerParams(vmem_limit_bytes=VMEM_LIMIT),
        cost_estimate=pl.CostEstimate(
            flops=4 * owned * listed * width * width * half,
            bytes_accessed=4 * m.size + 6 * near.size,
            transcendentals=0,
        ),
        name="metric",
    )(mine_cols, peer_cols, near, even, odd, m, pm)


def build_kernel(owned, half, pieces, tile_ref, domain_ref, number_ref, t_ref, *rest):
    piece_refs, (out_ref, table, sems) = rest[: 2 * pieces], rest[2 * pieces :]
    step = pl.program_id(0)
    me = lax.axis_index("space")
    mine = lax.axis_index("sub")

    @pl.when(step == 0)
    def _():
        copies = []
        for k in range(pieces):
            for side in range(2):
                start = mine * half if side == 0 else (1 - mine) * half
                copies.append(
                    pltpu.make_async_copy(
                        piece_refs[side * pieces + k],
                        table.at[pl.ds(k * owned, owned), pl.ds(pl.multiple_of(start, half), half), :],
                        sems.at[side * pieces + k],
                    )
                )
        for copy in copies:
            copy.start()
        for copy in copies:
            copy.wait()

    left, right = [], []
    for k in range(t_ref.shape[1]):
        touched = tile_ref[step, k]
        slot = jnp.bitwise_xor(domain_ref[touched], me) * owned + number_ref[touched]
        left.append(t_ref[0, k])
        right.append(table[slot])
    out_ref[0] = lax.dot_general(
        jnp.concatenate(left, axis=1), jnp.concatenate(right, axis=1), NT, preferred_element_type=F32
    ).astype(out_ref.dtype)


def build(block_tile, domain, number, three_centre, pieces, ahead, parts, name):
    blocks, listed, width, _ = three_centre.shape
    owned, half, _ = pieces[0].shape
    count = len(pieces) // 2
    rows = width // parts
    columns = 2 * half
    return pl.pallas_call(
        functools.partial(build_kernel, owned, half, count),
        grid_spec=pltpu.PrefetchScalarGridSpec(
            num_scalar_prefetch=3,
            grid=(blocks,),
            in_specs=[
                pl.BlockSpec(
                    (1, listed, rows, width),
                    lambda p, *_: (p, 0, lax.rem(lax.axis_index("aux") + ahead, parts), 0),
                )
            ]
            + [pl.BlockSpec(memory_space=pl.ANY)] * len(pieces),
            out_specs=pl.BlockSpec((1, rows, columns), lambda p, *_: (p, 0, 0)),
            scratch_shapes=[
                pltpu.VMEM((count * owned, columns, width), BF16),
                pltpu.SemaphoreType.DMA((len(pieces),)),
            ],
        ),
        out_shape=jax.ShapeDtypeStruct((blocks, rows, columns), BF16),
        compiler_params=pltpu.CompilerParams(vmem_limit_bytes=VMEM_LIMIT),
        cost_estimate=pl.CostEstimate(
            flops=2 * blocks * listed * width * rows * columns,
            bytes_accessed=2 * (three_centre.size // parts + blocks * rows * columns),
            transcendentals=0,
        ),
        name=name,
    )(block_tile, domain, number, three_centre, *pieces)


def exchange(array, axis, distance):
    return lax.ppermute(array, axis, [(i, i ^ distance) for i in range(lax.axis_size(axis))])


def ahead_by(array, axis, distance):
    count = lax.axis_size(axis)
    return lax.ppermute(array, axis, [(i, (i + distance) % count) for i in range(count)])


def pairs_from(array, axis, first):
    swaps = []
    for low in range(first, lax.axis_size(axis) - 1, 2):
        swaps += [(low, low + 1), (low + 1, low)]
    return lax.ppermute(array, axis, swaps)


def shards(
    densities, three_centre, block_tile, owner_domain, owner_tile, metric_inverse, metric_columns
):
    domains = lax.axis_size("space")
    aux_count = lax.axis_size("aux")
    touched = owner_tile.shape[-1]
    owned, _, width, _ = metric_inverse.shape
    half = densities.shape[2] // 2
    domain = owner_domain.reshape(touched)
    number = owner_tile.reshape(touched)

    peer_metric = exchange(metric_inverse, "sub", 1)
    peer_columns = exchange(metric_columns, "sub", 1)

    keep, send = fit(block_tile, domain, number, densities, three_centre, domains, owned)
    got = exchange(send, "sub", 1)
    chip = (keep.astype(F32) + got.astype(F32)).astype(BF16).reshape(domains, owned, half, width)
    arrived = [exchange(chip[k], "space", k) for k in range(1, domains)]
    total = chip[0].astype(F32)
    for piece in arrived:
        total = total + piece.astype(F32)
    fitted = total.astype(BF16)

    near = jnp.concatenate(
        [fitted] + [ahead_by(fitted, "aux", aux_count - k) for k in range(1, aux_count)]
    )
    even = pairs_from(near, "space", 0)
    odd = pairs_from(near, "space", 1)
    coefficients = metric(
        metric_columns, peer_columns, near, even, odd, metric_inverse, peer_metric, aux_count
    )

    pieces = [coefficients] + [exchange(coefficients, "space", k) for k in range(1, domains)]
    pieces = pieces + [exchange(piece, "sub", 1) for piece in pieces]

    rows = []
    for ahead in list(range(1, aux_count)) + [0]:
        part = build(block_tile, domain, number, three_centre, pieces, ahead, aux_count, f"build_{ahead}")
        rows.append(ahead_by(part, "aux", ahead) if ahead else part)
    result = rows[-1].astype(F32)
    for part in rows[:-1]:
        result = result + part.astype(F32)
    return result.astype(BF16)


def solution(mesh):
    placed = (
        P(("frag", "space", "sub"), None, None),
        P(("frag", "space", "sub"), "aux", None, None),
        P(("frag", "space", "sub"), "aux"),
        P(("frag", "space", "sub"), "aux", None, None),
        P(("frag", "space", "sub"), "aux", None),
        P(("frag", "space", "aux"), "sub", None, None),
        P(("frag", "space", "aux"), "sub"),
    )
    return jax.shard_map(
        shards,
        mesh=mesh,
        in_specs=placed,
        out_specs=P(("frag", "space", "sub"), "aux", None),
        check_vma=False,
    )
```

```python
import functools

import jax
import jax.numpy as jnp
from jax import lax
from jax.experimental import pallas as pl
from jax.experimental.pallas import tpu as pltpu
from jax.sharding import PartitionSpec as P

BF16 = jnp.bfloat16
F32 = jnp.float32
NT = (((1,), (1,)), ((), ()))
VMEM_LIMIT = 32 * 1024 * 1024
FIT_VMEM_LIMIT = 56 * 1024 * 1024
VMEM = pl.BlockSpec(memory_space=pltpu.VMEM)
SMEM = pl.BlockSpec(memory_space=pltpu.SMEM)


def fit_kernel(
    owned, half, tile_hbm, domain_hbm, number_hbm, d_hbm, t_hbm, keep_ref, send_ref, slot_ref,
    acc, tile_ref, domain_ref, number_ref, d_ref, t_ref, small_sem, d_sem, t_sem,
):
    me = lax.axis_index("space")
    mine = lax.axis_index("sub")
    blocks, listed = t_ref.shape[:2]
    small = [
        pltpu.make_async_copy(tile_hbm, tile_ref, small_sem.at[0]),
        pltpu.make_async_copy(domain_hbm, domain_ref, small_sem.at[1]),
        pltpu.make_async_copy(number_hbm, number_ref, small_sem.at[2]),
    ]
    d_copies = [pltpu.make_async_copy(d_hbm.at[p], d_ref.at[p], d_sem.at[p]) for p in range(blocks)]
    t_copies = [pltpu.make_async_copy(t_hbm.at[p], t_ref.at[p], t_sem.at[p]) for p in range(blocks)]
    for copy in small:
        copy.start()
    for p in range(blocks):
        d_copies[p].start()
        t_copies[p].start()
    acc[...] = jnp.zeros_like(acc)
    for copy in small:
        copy.wait()
    for p in range(blocks):
        d_copies[p].wait()
        rows = jnp.transpose(d_ref[p])
        t_copies[p].wait()
        for k in range(listed):
            touched = tile_ref[p, k]
            slot = jnp.bitwise_xor(domain_ref[touched], me) * owned + number_ref[touched]
            slot_ref[p, k] = slot
            acc[slot] += jnp.dot(rows, t_ref[p, k], preferred_element_type=F32)
    keep_ref[...] = acc[:, pl.ds(pl.multiple_of(mine * half, half), half), :].astype(BF16)
    send_ref[...] = acc[:, pl.ds(pl.multiple_of((1 - mine) * half, half), half), :].astype(BF16)


def fit(block_tile, domain, number, densities, three_centre, domains, owned):
    blocks, listed, width, _ = three_centre.shape
    columns = densities.shape[2]
    half = columns // 2
    slots = domains * owned
    out = jax.ShapeDtypeStruct((slots, half, width), BF16)
    return pl.pallas_call(
        functools.partial(fit_kernel, owned, half),
        in_specs=[pl.BlockSpec(memory_space=pltpu.HBM)] * 5,
        out_specs=[VMEM, VMEM, SMEM],
        scratch_shapes=[
            pltpu.VMEM((slots, columns, width), F32),
            pltpu.SMEM(block_tile.shape, jnp.int32),
            pltpu.SMEM(domain.shape, jnp.int32),
            pltpu.SMEM(number.shape, jnp.int32),
            pltpu.VMEM(densities.shape, BF16),
            pltpu.VMEM(three_centre.shape, BF16),
            pltpu.SemaphoreType.DMA((3,)),
            pltpu.SemaphoreType.DMA((blocks,)),
            pltpu.SemaphoreType.DMA((blocks,)),
        ],
        out_shape=[out, out, jax.ShapeDtypeStruct(block_tile.shape, jnp.int32)],
        compiler_params=pltpu.CompilerParams(vmem_limit_bytes=FIT_VMEM_LIMIT),
        cost_estimate=pl.CostEstimate(
            flops=2 * blocks * listed * width * width * columns,
            bytes_accessed=2 * (three_centre.size + densities.size),
            transcendentals=0,
        ),
        name="fit",
    )(block_tile, domain, number, densities, three_centre)


def metric_kernel(owned, count, mine_cols, peer_cols, near_ref, even_ref, odd_ref, m_ref, pm_ref, out_ref, window):
    me = lax.axis_index("space")
    aux = lax.axis_index("aux")
    own = owned * count
    window[:own] = near_ref[...]
    window[own : 2 * own] = even_ref[...]
    window[2 * own :] = odd_ref[...]

    def place(column):
        zone = column // own
        rest = column % own
        side = jnp.where((zone == 2) == (me % 2 == 0), 1, 2)
        block = jnp.where(zone == 1, 0, side)
        turned = (rest // owned + count - aux) % count
        return block * own + turned * owned + rest % owned

    for q in range(m_ref.shape[0]):
        picked, blocks = [], []
        for cols, mat in ((mine_cols, m_ref), (peer_cols, pm_ref)):
            for m in range(mat.shape[1]):
                picked.append(window[place(cols[q, m])])
                blocks.append(mat[q, m])
        out_ref[q] = lax.dot_general(
            jnp.concatenate(picked, axis=1),
            jnp.concatenate(blocks, axis=1),
            NT,
            preferred_element_type=F32,
        ).astype(BF16)


def metric(mine_cols, peer_cols, near, even, odd, m, pm, count):
    owned, listed, width, _ = m.shape
    half = near.shape[1]
    return pl.pallas_call(
        functools.partial(metric_kernel, owned, count),
        in_specs=[SMEM] * 2 + [VMEM] * 5,
        out_specs=VMEM,
        out_shape=jax.ShapeDtypeStruct((owned, half, width), BF16),
        scratch_shapes=[pltpu.VMEM((3 * owned * count, half, width), BF16)],
        compiler_params=pltpu.CompilerParams(vmem_limit_bytes=VMEM_LIMIT),
        cost_estimate=pl.CostEstimate(
            flops=4 * owned * listed * width * width * half,
            bytes_accessed=4 * m.size + 6 * near.size,
            transcendentals=0,
        ),
        name="metric",
    )(mine_cols, peer_cols, near, even, odd, m, pm)


def build_kernel(parts, slot_ref, t_ref, *rest):
    piece_refs, (out_ref, table) = rest[:-2], rest[-2:]
    aux = lax.axis_index("aux")
    blocks, listed, width, _ = t_ref.shape
    owned = piece_refs[0].shape[0]
    rows = width // parts
    for k, piece in enumerate(piece_refs):
        table[k * owned : (k + 1) * owned] = piece[...]
    for p in range(blocks):
        left = [t_ref[p, k] for k in range(listed)]
        right = [table[slot_ref[p, k]] for k in range(listed)]
        total = lax.dot_general(
            jnp.concatenate(left, axis=1), jnp.concatenate(right, axis=1), NT, preferred_element_type=F32
        ).astype(BF16)
        for part in range(parts):
            out_ref[lax.rem(part + parts - aux, parts), p] = total[part * rows : (part + 1) * rows]


def build(slots, three_centre, pieces, parts, name):
    blocks, listed, width, _ = three_centre.shape
    owned, half, _ = pieces[0].shape
    return pl.pallas_call(
        functools.partial(build_kernel, parts),
        in_specs=[SMEM] + [VMEM] * (1 + len(pieces)),
        out_specs=VMEM,
        out_shape=jax.ShapeDtypeStruct((parts, blocks, width // parts, half), BF16),
        scratch_shapes=[pltpu.VMEM((len(pieces) * owned, half, width), BF16)],
        compiler_params=pltpu.CompilerParams(vmem_limit_bytes=VMEM_LIMIT),
        cost_estimate=pl.CostEstimate(
            flops=2 * blocks * listed * width * width * half,
            bytes_accessed=2 * (three_centre.size + blocks * width * half),
            transcendentals=0,
        ),
        name=name,
    )(slots, three_centre, *pieces)


def exchange(array, axis, distance):
    return lax.ppermute(array, axis, [(i, i ^ distance) for i in range(lax.axis_size(axis))])


def ahead_by(array, axis, distance):
    count = lax.axis_size(axis)
    return lax.ppermute(array, axis, [(i, (i + distance) % count) for i in range(count)])


def pairs_from(array, axis, first):
    swaps = []
    for low in range(first, lax.axis_size(axis) - 1, 2):
        swaps += [(low, low + 1), (low + 1, low)]
    return lax.ppermute(array, axis, swaps)


def shards(
    densities, three_centre, block_tile, owner_domain, owner_tile, metric_inverse, metric_columns
):
    domains = lax.axis_size("space")
    aux_count = lax.axis_size("aux")
    touched = owner_tile.shape[-1]
    owned, _, width, _ = metric_inverse.shape
    half = densities.shape[2] // 2
    domain = owner_domain.reshape(touched)
    number = owner_tile.reshape(touched)

    keep, send, slots = fit(block_tile, domain, number, densities, three_centre, domains, owned)
    got = exchange(send, "sub", 1)
    chip = (keep.astype(F32) + got.astype(F32)).astype(BF16).reshape(domains, owned, half, width)
    chip, own_metric, own_columns = lax.optimization_barrier((chip, metric_inverse, metric_columns))
    arrived = [exchange(chip[k], "space", k) for k in range(1, domains)]
    peer_metric = exchange(own_metric, "sub", 1)
    peer_columns = exchange(own_columns, "sub", 1)
    arrived, peer_metric, peer_columns = lax.optimization_barrier((arrived, peer_metric, peer_columns))
    total = chip[0].astype(F32)
    for piece in arrived:
        total = total + piece.astype(F32)
    fitted = total.astype(BF16)

    near = jnp.concatenate(
        [fitted] + [ahead_by(fitted, "aux", aux_count - k) for k in range(1, aux_count)]
    )
    even = pairs_from(near, "space", 0)
    odd = pairs_from(near, "space", 1)
    coefficients = metric(
        metric_columns, peer_columns, near, even, odd, metric_inverse, peer_metric, aux_count
    )

    pieces = [coefficients] + [exchange(coefficients, "space", k) for k in range(1, domains)]
    other = [exchange(piece, "sub", 1) for piece in pieces]

    sums = []
    for name, tiles in (("build_own", pieces), ("build_other", other)):
        parts = build(slots, three_centre, tiles, aux_count, name)
        terms = [parts[0]] + [ahead_by(parts[k], "aux", k) for k in range(1, aux_count)]
        sums.append(sum(term.astype(F32) for term in terms).astype(BF16))
    first = lax.axis_index("sub") == 0
    low, high = jnp.where(first, sums[0], sums[1]), jnp.where(first, sums[1], sums[0])
    return jnp.concatenate([low, high], axis=2)


def solution(mesh):
    placed = (
        P(("frag", "space", "sub"), None, None),
        P(("frag", "space", "sub"), "aux", None, None),
        P(("frag", "space", "sub"), "aux"),
        P(("frag", "space", "sub"), "aux", None, None),
        P(("frag", "space", "sub"), "aux", None),
        P(("frag", "space", "aux"), "sub", None, None),
        P(("frag", "space", "aux"), "sub"),
    )
    return jax.shard_map(
        shards,
        mesh=mesh,
        in_specs=placed,
        out_specs=P(("frag", "space", "sub"), "aux", None),
        check_vma=False,
    )
```

```python
import functools

import jax
import jax.numpy as jnp
from jax import lax
from jax.experimental import pallas as pl
from jax.experimental.pallas import tpu as pltpu
from jax.sharding import PartitionSpec as P

BF16 = jnp.bfloat16
F32 = jnp.float32
NT = (((1,), (1,)), ((), ()))
VMEM_LIMIT = 32 * 1024 * 1024
FIT_VMEM_LIMIT = 53 * 1024 * 1024
VMEM = pl.BlockSpec(memory_space=pltpu.VMEM)
SMEM = pl.BlockSpec(memory_space=pltpu.SMEM)


def fit_kernel(
    owned, half, groups, table_ref, d_hbm, t_hbm, keep_ref, send_ref, slot_ref, acc, d_ref, t_ref, d_sem, t_sem
):
    me = lax.axis_index("space")
    mine = lax.axis_index("sub")
    blocks, listed = t_ref.shape[:2]
    copies, begin = [], 0
    for i, size in enumerate(groups):
        part = pl.ds(begin, size)
        copies.append(
            (
                pltpu.make_async_copy(d_hbm.at[part], d_ref.at[part], d_sem.at[i]),
                pltpu.make_async_copy(t_hbm.at[part], t_ref.at[part], t_sem.at[i]),
            )
        )
        begin += size
    for pair in copies:
        for copy in pair:
            copy.start()
    acc[...] = jnp.zeros_like(acc)
    begin = 0
    for size, pair in zip(groups, copies):
        for copy in pair:
            copy.wait()
        for p in range(begin, begin + size):
            rows = jnp.transpose(d_ref[p])
            for k in range(listed):
                touched = table_ref[p, k]
                slot = jnp.bitwise_xor(table_ref[blocks, touched], me) * owned + table_ref[blocks + 1, touched]
                slot_ref[p, k] = slot
                acc[slot] += jnp.dot(rows, t_ref[p, k], preferred_element_type=F32)
        begin += size
    keep_ref[...] = acc[:, pl.ds(pl.multiple_of(mine * half, half), half), :].astype(BF16)
    send_ref[...] = acc[:, pl.ds(pl.multiple_of((1 - mine) * half, half), half), :].astype(BF16)


def fit(tables, densities, three_centre, domains, owned):
    blocks, listed, width, _ = three_centre.shape
    columns = densities.shape[2]
    half = columns // 2
    count = domains * owned
    groups = (blocks // 4, blocks // 4, blocks - 2 * (blocks // 4))
    out = jax.ShapeDtypeStruct((count, half, width), BF16)
    return pl.pallas_call(
        functools.partial(fit_kernel, owned, half, groups),
        in_specs=[SMEM] + [pl.BlockSpec(memory_space=pltpu.HBM)] * 2,
        out_specs=[VMEM, VMEM, SMEM],
        scratch_shapes=[
            pltpu.VMEM((count, columns, width), F32),
            pltpu.VMEM(densities.shape, BF16),
            pltpu.VMEM(three_centre.shape, BF16),
            pltpu.SemaphoreType.DMA((len(groups),)),
            pltpu.SemaphoreType.DMA((len(groups),)),
        ],
        out_shape=[out, out, jax.ShapeDtypeStruct((blocks, listed), jnp.int32)],
        compiler_params=pltpu.CompilerParams(vmem_limit_bytes=FIT_VMEM_LIMIT),
        cost_estimate=pl.CostEstimate(
            flops=2 * blocks * listed * width * width * columns,
            bytes_accessed=2 * (three_centre.size + densities.size),
            transcendentals=0,
        ),
        name="fit",
    )(tables, densities, three_centre)


def metric_kernel(owned, count, mine_cols, peer_cols, near_ref, odd_ref, even_ref, m_ref, pm_ref, out_ref, window):
    me = lax.axis_index("space")
    aux = lax.axis_index("aux")
    own = owned * count
    window[:own] = near_ref[...]
    window[own : 2 * own] = even_ref[...]
    window[2 * own :] = odd_ref[...]

    def place(column):
        zone = column // own
        rest = column % own
        side = jnp.where((zone == 2) == (me % 2 == 0), 1, 2)
        block = jnp.where(zone == 1, 0, side)
        turned = (rest // owned + count - aux) % count
        return block * own + turned * owned + rest % owned

    for q in range(m_ref.shape[0]):
        picked, blocks = [], []
        for cols, mat in ((mine_cols, m_ref), (peer_cols, pm_ref)):
            for m in range(mat.shape[1]):
                picked.append(window[place(cols[q, m])])
                blocks.append(mat[q, m])
        out_ref[q] = lax.dot_general(
            jnp.concatenate(picked, axis=1),
            jnp.concatenate(blocks, axis=1),
            NT,
            preferred_element_type=F32,
        ).astype(BF16)


def metric(mine_cols, peer_cols, near, odd, even, m, pm, count):
    owned, listed, width, _ = m.shape
    half = near.shape[1]
    return pl.pallas_call(
        functools.partial(metric_kernel, owned, count),
        in_specs=[SMEM] * 2 + [VMEM] * 5,
        out_specs=VMEM,
        out_shape=jax.ShapeDtypeStruct((owned, half, width), BF16),
        scratch_shapes=[pltpu.VMEM((3 * owned * count, half, width), BF16)],
        compiler_params=pltpu.CompilerParams(vmem_limit_bytes=VMEM_LIMIT),
        cost_estimate=pl.CostEstimate(
            flops=4 * owned * listed * width * width * half,
            bytes_accessed=4 * m.size + 6 * near.size,
            transcendentals=0,
        ),
        name="metric",
    )(mine_cols, peer_cols, near, odd, even, m, pm)


def build_kernel(parts, slot_ref, t_ref, *rest):
    piece_refs, (out_ref, table) = rest[:-2], rest[-2:]
    aux = lax.axis_index("aux")
    blocks, listed, width, _ = t_ref.shape
    owned = piece_refs[0].shape[0]
    rows = width // parts
    for k, piece in enumerate(piece_refs):
        table[k * owned : (k + 1) * owned] = piece[...]
    for p in range(blocks):
        left = [t_ref[p, k] for k in range(listed)]
        right = [table[slot_ref[p, k]] for k in range(listed)]
        total = lax.dot_general(
            jnp.concatenate(left, axis=1), jnp.concatenate(right, axis=1), NT, preferred_element_type=F32
        ).astype(BF16)
        for part in range(parts):
            out_ref[lax.rem(part + parts - aux, parts), p] = total[part * rows : (part + 1) * rows]


def build(slots, three_centre, pieces, parts, name):
    blocks, listed, width, _ = three_centre.shape
    owned, half, _ = pieces[0].shape
    return pl.pallas_call(
        functools.partial(build_kernel, parts),
        in_specs=[SMEM] + [VMEM] * (1 + len(pieces)),
        out_specs=VMEM,
        out_shape=jax.ShapeDtypeStruct((parts, blocks, width // parts, half), BF16),
        scratch_shapes=[pltpu.VMEM((len(pieces) * owned, half, width), BF16)],
        compiler_params=pltpu.CompilerParams(vmem_limit_bytes=VMEM_LIMIT),
        cost_estimate=pl.CostEstimate(
            flops=2 * blocks * listed * width * width * half,
            bytes_accessed=2 * (three_centre.size + blocks * width * half),
            transcendentals=0,
        ),
        name=name,
    )(slots, three_centre, *pieces)


def exchange(array, axis, distance):
    return lax.ppermute(array, axis, [(i, i ^ distance) for i in range(lax.axis_size(axis))])


def ahead_by(array, axis, distance):
    count = lax.axis_size(axis)
    return lax.ppermute(array, axis, [(i, (i + distance) % count) for i in range(count)])


def pairs_from(array, axis, first):
    swaps = []
    for low in range(first, lax.axis_size(axis) - 1, 2):
        swaps += [(low, low + 1), (low + 1, low)]
    return lax.ppermute(array, axis, swaps)


def shards(
    densities, three_centre, block_tile, owner_domain, owner_tile, metric_inverse, metric_columns
):
    domains = lax.axis_size("space")
    aux_count = lax.axis_size("aux")
    touched = owner_tile.shape[-1]
    owned, _, width, _ = metric_inverse.shape
    half = densities.shape[2] // 2
    domain = owner_domain.reshape(touched)
    number = owner_tile.reshape(touched)

    wide = max(touched, block_tile.shape[1])
    tables = jnp.concatenate(
        [jnp.pad(row, ((0, 0), (0, wide - row.shape[1]))) for row in (block_tile, domain[None], number[None])]
    )
    keep, send, slots = fit(tables, densities, three_centre, domains, owned)
    got = exchange(send, "sub", 1)
    chip = (keep.astype(F32) + got.astype(F32)).astype(BF16).reshape(domains, owned, half, width)
    chip, own_metric, own_columns = lax.optimization_barrier((chip, metric_inverse, metric_columns))
    arrived = [exchange(chip[k], "space", k) for k in range(1, domains)]
    peer_metric = exchange(own_metric, "sub", 1)
    peer_columns = exchange(own_columns, "sub", 1)
    arrived, peer_metric, peer_columns = lax.optimization_barrier((arrived, peer_metric, peer_columns))
    total = chip[0].astype(F32)
    for piece in arrived:
        total = total + piece.astype(F32)
    fitted = total.astype(BF16)

    near = jnp.concatenate(
        [fitted] + [ahead_by(fitted, "aux", aux_count - k) for k in range(1, aux_count)]
    )
    odd = pairs_from(near, "space", 1)
    even = pairs_from(near, "space", 0)
    coefficients = metric(
        metric_columns, peer_columns, near, odd, even, metric_inverse, peer_metric, aux_count
    )

    pieces = [coefficients] + [exchange(coefficients, "space", k) for k in range(1, domains)]
    other = [exchange(piece, "sub", 1) for piece in pieces]

    sums = []
    for name, tiles in (("build_own", pieces), ("build_other", other)):
        parts = build(slots, three_centre, tiles, aux_count, name)
        terms = [parts[0]] + [ahead_by(parts[k], "aux", k) for k in range(1, aux_count)]
        sums.append(sum(term.astype(F32) for term in terms).astype(BF16))
    first = lax.axis_index("sub") == 0
    low, high = jnp.where(first, sums[0], sums[1]), jnp.where(first, sums[1], sums[0])
    return jnp.concatenate([low, high], axis=2)


def solution(mesh):
    placed = (
        P(("frag", "space", "sub"), None, None),
        P(("frag", "space", "sub"), "aux", None, None),
        P(("frag", "space", "sub"), "aux"),
        P(("frag", "space", "sub"), "aux", None, None),
        P(("frag", "space", "sub"), "aux", None),
        P(("frag", "space", "aux"), "sub", None, None),
        P(("frag", "space", "aux"), "sub"),
    )
    return jax.shard_map(
        shards,
        mesh=mesh,
        in_specs=placed,
        out_specs=P(("frag", "space", "sub"), "aux", None),
        check_vma=False,
    )
```

```python
import functools

import jax
import jax.numpy as jnp
from jax import lax
from jax.experimental import pallas as pl
from jax.experimental.pallas import tpu as pltpu
from jax.sharding import PartitionSpec as P

BF16 = jnp.bfloat16
F32 = jnp.float32
NT = (((1,), (1,)), ((), ()))
VMEM_LIMIT = 32 * 1024 * 1024
FIT_VMEM_LIMIT = 53 * 1024 * 1024
VMEM = pl.BlockSpec(memory_space=pltpu.VMEM)
SMEM = pl.BlockSpec(memory_space=pltpu.SMEM)


def fit_kernel(
    owned, half, groups, table_ref, d_hbm, t_hbm, keep_ref, send_ref, slot_ref, acc, d_ref, t_ref, d_sem, t_sem
):
    me = lax.axis_index("space")
    mine = lax.axis_index("sub")
    blocks, listed = t_ref.shape[:2]
    copies, begin = [], 0
    for i, size in enumerate(groups):
        part = pl.ds(begin, size)
        copies.append(
            (
                pltpu.make_async_copy(d_hbm.at[part], d_ref.at[part], d_sem.at[i]),
                pltpu.make_async_copy(t_hbm.at[part], t_ref.at[part], t_sem.at[i]),
            )
        )
        begin += size
    for pair in copies:
        for copy in pair:
            copy.start()
    acc[...] = jnp.zeros_like(acc)
    begin = 0
    for size, pair in zip(groups, copies):
        for copy in pair:
            copy.wait()
        for p in range(begin, begin + size):
            rows = jnp.transpose(d_ref[p])
            for k in range(listed):
                touched = table_ref[p, k]
                slot = jnp.bitwise_xor(table_ref[blocks, touched], me) * owned + table_ref[blocks + 1, touched]
                slot_ref[p, k] = slot
                acc[slot] += jnp.dot(rows, t_ref[p, k], preferred_element_type=F32)
        begin += size
    keep_ref[...] = acc[:, pl.ds(pl.multiple_of(mine * half, half), half), :].astype(BF16)
    send_ref[...] = acc[:, pl.ds(pl.multiple_of((1 - mine) * half, half), half), :].astype(BF16)


def fit(tables, densities, three_centre, domains, owned):
    blocks, listed, width, _ = three_centre.shape
    columns = densities.shape[2]
    half = columns // 2
    count = domains * owned
    groups = (blocks // 4, blocks // 4, blocks - 2 * (blocks // 4))
    out = jax.ShapeDtypeStruct((count, half, width), BF16)
    return pl.pallas_call(
        functools.partial(fit_kernel, owned, half, groups),
        in_specs=[SMEM] + [pl.BlockSpec(memory_space=pltpu.HBM)] * 2,
        out_specs=[VMEM, VMEM, SMEM],
        scratch_shapes=[
            pltpu.VMEM((count, columns, width), F32),
            pltpu.VMEM(densities.shape, BF16),
            pltpu.VMEM(three_centre.shape, BF16),
            pltpu.SemaphoreType.DMA((len(groups),)),
            pltpu.SemaphoreType.DMA((len(groups),)),
        ],
        out_shape=[out, out, jax.ShapeDtypeStruct((blocks, listed), jnp.int32)],
        compiler_params=pltpu.CompilerParams(vmem_limit_bytes=FIT_VMEM_LIMIT),
        cost_estimate=pl.CostEstimate(
            flops=2 * blocks * listed * width * width * columns,
            bytes_accessed=2 * (three_centre.size + densities.size),
            transcendentals=0,
        ),
        name="fit",
    )(tables, densities, three_centre)


def metric_kernel(owned, count, mine_cols, peer_cols, near_ref, even_ref, odd_ref, m_ref, pm_ref, out_ref, window):
    me = lax.axis_index("space")
    aux = lax.axis_index("aux")
    own = owned * count
    window[:own] = near_ref[...]
    window[own : 2 * own] = even_ref[...]
    window[2 * own :] = odd_ref[...]

    def place(column):
        zone = column // own
        rest = column % own
        side = jnp.where((zone == 2) == (me % 2 == 0), 1, 2)
        block = jnp.where(zone == 1, 0, side)
        turned = (rest // owned + count - aux) % count
        return block * own + turned * owned + rest % owned

    for q in range(m_ref.shape[0]):
        picked, blocks = [], []
        for cols, mat in ((mine_cols, m_ref), (peer_cols, pm_ref)):
            for m in range(mat.shape[1]):
                picked.append(window[place(cols[q, m])])
                blocks.append(mat[q, m])
        out_ref[q] = lax.dot_general(
            jnp.concatenate(picked, axis=1),
            jnp.concatenate(blocks, axis=1),
            NT,
            preferred_element_type=F32,
        ).astype(BF16)


def metric(mine_cols, peer_cols, near, even, odd, m, pm, count):
    owned, listed, width, _ = m.shape
    half = near.shape[1]
    return pl.pallas_call(
        functools.partial(metric_kernel, owned, count),
        in_specs=[SMEM] * 2 + [VMEM] * 5,
        out_specs=VMEM,
        out_shape=jax.ShapeDtypeStruct((owned, half, width), BF16),
        scratch_shapes=[pltpu.VMEM((3 * owned * count, half, width), BF16)],
        compiler_params=pltpu.CompilerParams(vmem_limit_bytes=VMEM_LIMIT),
        cost_estimate=pl.CostEstimate(
            flops=4 * owned * listed * width * width * half,
            bytes_accessed=4 * m.size + 6 * near.size,
            transcendentals=0,
        ),
        name="metric",
    )(mine_cols, peer_cols, near, even, odd, m, pm)


def build_kernel(parts, order, slot_ref, t_ref, *rest):
    piece_refs, (out_ref, table) = rest[:-2], rest[-2:]
    aux = lax.axis_index("aux")
    blocks, listed, width, _ = t_ref.shape
    owned = piece_refs[0].shape[0]
    rows = width // parts
    for k, piece in zip(order, piece_refs):
        table[k * owned : (k + 1) * owned] = piece[...]
    for p in range(blocks):
        left = [t_ref[p, k] for k in range(listed)]
        right = [table[slot_ref[p, k]] for k in range(listed)]
        total = lax.dot_general(
            jnp.concatenate(left, axis=1), jnp.concatenate(right, axis=1), NT, preferred_element_type=F32
        ).astype(BF16)
        for part in range(parts):
            out_ref[lax.rem(part + parts - aux, parts), p] = total[part * rows : (part + 1) * rows]


def build(slots, three_centre, pieces, order, parts, name):
    blocks, listed, width, _ = three_centre.shape
    owned, half, _ = pieces[0].shape
    return pl.pallas_call(
        functools.partial(build_kernel, parts, order),
        in_specs=[SMEM] + [VMEM] * (1 + len(pieces)),
        out_specs=VMEM,
        out_shape=jax.ShapeDtypeStruct((parts, blocks, width // parts, half), BF16),
        scratch_shapes=[pltpu.VMEM((len(pieces) * owned, half, width), BF16)],
        compiler_params=pltpu.CompilerParams(vmem_limit_bytes=VMEM_LIMIT),
        cost_estimate=pl.CostEstimate(
            flops=2 * blocks * listed * width * width * half,
            bytes_accessed=2 * (three_centre.size + blocks * width * half),
            transcendentals=0,
        ),
        name=name,
    )(slots, three_centre, *pieces)


def exchange(array, axis, distance):
    return lax.ppermute(array, axis, [(i, i ^ distance) for i in range(lax.axis_size(axis))])


def ahead_by(array, axis, distance):
    count = lax.axis_size(axis)
    return lax.ppermute(array, axis, [(i, (i + distance) % count) for i in range(count)])


def pairs_from(array, axis, first):
    swaps = []
    for low in range(first, lax.axis_size(axis) - 1, 2):
        swaps += [(low, low + 1), (low + 1, low)]
    return lax.ppermute(array, axis, swaps)


def shards(
    densities, three_centre, block_tile, owner_domain, owner_tile, metric_inverse, metric_columns
):
    domains = lax.axis_size("space")
    aux_count = lax.axis_size("aux")
    touched = owner_tile.shape[-1]
    owned, _, width, _ = metric_inverse.shape
    half = densities.shape[2] // 2
    domain = owner_domain.reshape(touched)
    number = owner_tile.reshape(touched)

    wide = max(touched, block_tile.shape[1])
    tables = jnp.concatenate(
        [jnp.pad(row, ((0, 0), (0, wide - row.shape[1]))) for row in (block_tile, domain[None], number[None])]
    )
    keep, send, slots = fit(tables, densities, three_centre, domains, owned)
    got = exchange(send, "sub", 1)
    chip = (keep.astype(F32) + got.astype(F32)).astype(BF16).reshape(domains, owned, half, width)
    chip, own_metric, own_columns = lax.optimization_barrier((chip, metric_inverse, metric_columns))
    arrived = [exchange(chip[k], "space", k) for k in range(1, domains)]
    peer_metric = exchange(own_metric, "sub", 1)
    peer_columns = exchange(own_columns, "sub", 1)
    arrived, peer_metric, peer_columns = lax.optimization_barrier((arrived, peer_metric, peer_columns))
    total = chip[0].astype(F32)
    for piece in arrived:
        total = total + piece.astype(F32)
    fitted = total.astype(BF16)

    near = jnp.concatenate(
        [fitted] + [ahead_by(fitted, "aux", aux_count - k) for k in range(1, aux_count)]
    )
    even = pairs_from(near, "space", 0)
    odd = pairs_from(near, "space", 1)
    coefficients = metric(
        metric_columns, peer_columns, near, even, odd, metric_inverse, peer_metric, aux_count
    )

    order = [0] + list(range(domains - 1, 0, -1))
    pieces = [coefficients] + [exchange(coefficients, "space", k) for k in order[1:]]
    other = [exchange(piece, "sub", 1) for piece in pieces]

    sums = []
    for name, tiles in (("build_own", pieces), ("build_other", other)):
        parts = build(slots, three_centre, tiles, order, aux_count, name)
        terms = [parts[0]] + [ahead_by(parts[k], "aux", k) for k in range(1, aux_count)]
        sums.append(sum(term.astype(F32) for term in terms).astype(BF16))
    first = lax.axis_index("sub") == 0
    low, high = jnp.where(first, sums[0], sums[1]), jnp.where(first, sums[1], sums[0])
    return jnp.concatenate([low, high], axis=2)


def solution(mesh):
    placed = (
        P(("frag", "space", "sub"), None, None),
        P(("frag", "space", "sub"), "aux", None, None),
        P(("frag", "space", "sub"), "aux"),
        P(("frag", "space", "sub"), "aux", None, None),
        P(("frag", "space", "sub"), "aux", None),
        P(("frag", "space", "aux"), "sub", None, None),
        P(("frag", "space", "aux"), "sub"),
    )
    return jax.shard_map(
        shards,
        mesh=mesh,
        in_specs=placed,
        out_specs=P(("frag", "space", "sub"), "aux", None),
        check_vma=False,
    )
```

```python
import functools

import jax
import jax.numpy as jnp
from jax import lax
from jax.experimental import pallas as pl
from jax.experimental.pallas import tpu as pltpu
from jax.sharding import PartitionSpec as P

BF16 = jnp.bfloat16
F32 = jnp.float32
NT = (((1,), (1,)), ((), ()))
VMEM_LIMIT = 32 * 1024 * 1024
VMEM = pl.BlockSpec(memory_space=pltpu.VMEM)
SMEM = pl.BlockSpec(memory_space=pltpu.SMEM)
ANY = pl.BlockSpec(memory_space=pl.ANY)


def fit_kernel(
    owned, half, groups, tile_hbm, domain_hbm, number_hbm, d_hbm, t_hbm, keep_ref, send_ref, slot_any,
    acc, tile_ref, domain_ref, number_ref, slot_ref, d_ref, t_ref, small_sem, d_sem, t_sem,
):
    me = lax.axis_index("space")
    mine = lax.axis_index("sub")
    blocks, listed = t_ref.shape[:2]
    small = [
        pltpu.make_async_copy(tile_hbm, tile_ref, small_sem.at[0]),
        pltpu.make_async_copy(domain_hbm, domain_ref, small_sem.at[1]),
        pltpu.make_async_copy(number_hbm, number_ref, small_sem.at[2]),
    ]
    for copy in small:
        copy.start()
    copies, begin = [], 0
    for i, size in enumerate(groups):
        part = pl.ds(begin, size)
        copies.append(
            (
                pltpu.make_async_copy(d_hbm.at[part], d_ref.at[part], d_sem.at[i]),
                pltpu.make_async_copy(t_hbm.at[part], t_ref.at[part], t_sem.at[i]),
            )
        )
        begin += size
    for pair in copies:
        for copy in pair:
            copy.start()
    acc[...] = jnp.zeros_like(acc)
    for copy in small:
        copy.wait()
    begin = 0
    for size, pair in zip(groups, copies):
        for copy in pair:
            copy.wait()
        for p in range(begin, begin + size):
            rows = jnp.transpose(d_ref[p])
            for k in range(listed):
                touched = tile_ref[p, k]
                slot = jnp.bitwise_xor(domain_ref[touched], me) * owned + number_ref[touched]
                slot_ref[p, k] = slot
                acc[slot] += jnp.dot(rows, t_ref[p, k], preferred_element_type=F32)
        begin += size
    slot_copy = pltpu.make_async_copy(slot_ref, slot_any, small_sem.at[3])
    slot_copy.start()
    keep_ref[...] = acc[:, pl.ds(pl.multiple_of(mine * half, half), half), :].astype(BF16)
    send_ref[...] = acc[:, pl.ds(pl.multiple_of((1 - mine) * half, half), half), :].astype(BF16)
    slot_copy.wait()


def fit(block_tile, domain, number, densities, three_centre, domains, owned):
    blocks, listed, width, _ = three_centre.shape
    columns = densities.shape[2]
    half = columns // 2
    count = domains * owned
    groups = (blocks // 4, 3 * blocks // 8, blocks - blocks // 4 - 3 * blocks // 8)
    out = jax.ShapeDtypeStruct((count, half, width), BF16)
    operands = (block_tile, domain, number, densities, three_centre)
    operands = [pltpu.with_memory_space_constraint(operand, pltpu.HBM) for operand in operands]
    return pl.pallas_call(
        functools.partial(fit_kernel, owned, half, groups),
        in_specs=[pl.BlockSpec(memory_space=pltpu.HBM)] * 5,
        out_specs=[VMEM, VMEM, ANY],
        scratch_shapes=[
            pltpu.VMEM((count, columns, width), F32),
            pltpu.SMEM(block_tile.shape, jnp.int32),
            pltpu.SMEM(domain.shape, jnp.int32),
            pltpu.SMEM(number.shape, jnp.int32),
            pltpu.SMEM(block_tile.shape, jnp.int32),
            pltpu.VMEM(densities.shape, BF16),
            pltpu.VMEM(three_centre.shape, BF16),
            pltpu.SemaphoreType.DMA((4,)),
            pltpu.SemaphoreType.DMA((len(groups),)),
            pltpu.SemaphoreType.DMA((len(groups),)),
        ],
        out_shape=[out, out, jax.ShapeDtypeStruct(block_tile.shape, jnp.int32)],
        compiler_params=pltpu.CompilerParams(vmem_limit_bytes=VMEM_LIMIT),
        cost_estimate=pl.CostEstimate(
            flops=2 * blocks * listed * width * width * columns,
            bytes_accessed=2 * (three_centre.size + densities.size),
            transcendentals=0,
        ),
        name="fit",
    )(*operands)


def metric_kernel(owned, count, mine_cols, peer_cols, near_ref, even_ref, odd_ref, m_ref, pm_ref, out_ref, window):
    me = lax.axis_index("space")
    aux = lax.axis_index("aux")
    own = owned * count
    window[:own] = near_ref[...]
    window[own : 2 * own] = even_ref[...]
    window[2 * own :] = odd_ref[...]

    def place(column):
        zone = column // own
        rest = column % own
        side = jnp.where((zone == 2) == (me % 2 == 0), 1, 2)
        block = jnp.where(zone == 1, 0, side)
        turned = (rest // owned + count - aux) % count
        return block * own + turned * owned + rest % owned

    for q in range(m_ref.shape[0]):
        picked, blocks = [], []
        for cols, mat in ((mine_cols, m_ref), (peer_cols, pm_ref)):
            for m in range(mat.shape[1]):
                picked.append(window[place(cols[q, m])])
                blocks.append(mat[q, m])
        out_ref[q] = lax.dot_general(
            jnp.concatenate(picked, axis=1),
            jnp.concatenate(blocks, axis=1),
            NT,
            preferred_element_type=F32,
        ).astype(BF16)


def metric(mine_cols, peer_cols, near, even, odd, m, pm, count):
    owned, listed, width, _ = m.shape
    half = near.shape[1]
    return pl.pallas_call(
        functools.partial(metric_kernel, owned, count),
        in_specs=[SMEM] * 2 + [VMEM] * 5,
        out_specs=VMEM,
        out_shape=jax.ShapeDtypeStruct((owned, half, width), BF16),
        scratch_shapes=[pltpu.VMEM((3 * owned * count, half, width), BF16)],
        compiler_params=pltpu.CompilerParams(vmem_limit_bytes=VMEM_LIMIT),
        cost_estimate=pl.CostEstimate(
            flops=4 * owned * listed * width * width * half,
            bytes_accessed=4 * m.size + 6 * near.size,
            transcendentals=0,
        ),
        name="metric",
    )(mine_cols, peer_cols, near, even, odd, m, pm)


def build_kernel(parts, order, slot_ref, t_ref, *rest):
    piece_refs, (out_ref, table) = rest[:-2], rest[-2:]
    aux = lax.axis_index("aux")
    blocks, listed, width, _ = t_ref.shape
    owned = piece_refs[0].shape[0]
    rows = width // parts
    for k, piece in zip(order, piece_refs):
        table[k * owned : (k + 1) * owned] = piece[...]
    for p in range(blocks):
        left = [t_ref[p, k] for k in range(listed)]
        right = [table[slot_ref[p, k]] for k in range(listed)]
        total = lax.dot_general(
            jnp.concatenate(left, axis=1), jnp.concatenate(right, axis=1), NT, preferred_element_type=F32
        ).astype(BF16)
        for part in range(parts):
            out_ref[lax.rem(part + parts - aux, parts), p] = total[part * rows : (part + 1) * rows]


def build(slots, three_centre, pieces, order, parts, name):
    blocks, listed, width, _ = three_centre.shape
    owned, half, _ = pieces[0].shape
    return pl.pallas_call(
        functools.partial(build_kernel, parts, order),
        in_specs=[SMEM] + [VMEM] * (1 + len(pieces)),
        out_specs=VMEM,
        out_shape=jax.ShapeDtypeStruct((parts, blocks, width // parts, half), BF16),
        scratch_shapes=[pltpu.VMEM((len(pieces) * owned, half, width), BF16)],
        compiler_params=pltpu.CompilerParams(vmem_limit_bytes=VMEM_LIMIT),
        cost_estimate=pl.CostEstimate(
            flops=2 * blocks * listed * width * width * half,
            bytes_accessed=2 * (three_centre.size + blocks * width * half),
            transcendentals=0,
        ),
        name=name,
    )(slots, three_centre, *pieces)


def exchange(array, axis, distance):
    return lax.ppermute(array, axis, [(i, i ^ distance) for i in range(lax.axis_size(axis))])


def ahead_by(array, axis, distance):
    count = lax.axis_size(axis)
    return lax.ppermute(array, axis, [(i, (i + distance) % count) for i in range(count)])


def pairs_from(array, axis, first):
    swaps = []
    for low in range(first, lax.axis_size(axis) - 1, 2):
        swaps += [(low, low + 1), (low + 1, low)]
    return lax.ppermute(array, axis, swaps)


def shards(
    densities, three_centre, block_tile, owner_domain, owner_tile, metric_inverse, metric_columns
):
    domains = lax.axis_size("space")
    aux_count = lax.axis_size("aux")
    touched = owner_tile.shape[-1]
    owned, _, width, _ = metric_inverse.shape
    half = densities.shape[2] // 2
    domain = owner_domain.reshape(touched)
    number = owner_tile.reshape(touched)

    keep, send, slots = fit(block_tile, domain, number, densities, three_centre, domains, owned)
    got = exchange(send, "sub", 1)
    chip = (keep.astype(F32) + got.astype(F32)).astype(BF16).reshape(domains, owned, half, width)
    chip, own_metric, own_columns = lax.optimization_barrier((chip, metric_inverse, metric_columns))
    arrived = [exchange(chip[k], "space", k) for k in range(1, domains)]
    peer_metric = exchange(own_metric, "sub", 1)
    peer_columns = exchange(own_columns, "sub", 1)
    arrived, peer_metric, peer_columns = lax.optimization_barrier((arrived, peer_metric, peer_columns))
    total = chip[0].astype(F32)
    for piece in arrived:
        total = total + piece.astype(F32)
    fitted = total.astype(BF16)

    near = jnp.concatenate(
        [fitted] + [ahead_by(fitted, "aux", aux_count - k) for k in range(1, aux_count)]
    )
    even = pairs_from(near, "space", 0)
    odd = pairs_from(near, "space", 1)
    coefficients = metric(
        metric_columns, peer_columns, near, even, odd, metric_inverse, peer_metric, aux_count
    )

    order = [0] + list(range(domains - 1, 0, -1))
    pieces = [coefficients] + [exchange(coefficients, "space", k) for k in order[1:]]
    other = [exchange(piece, "sub", 1) for piece in pieces]

    sums = []
    for name, tiles in (("build_own", pieces), ("build_other", other)):
        parts = build(slots, three_centre, tiles, order, aux_count, name)
        terms = [parts[0]] + [ahead_by(parts[k], "aux", k) for k in range(1, aux_count)]
        sums.append(sum(term.astype(F32) for term in terms).astype(BF16))
    first = lax.axis_index("sub") == 0
    low, high = jnp.where(first, sums[0], sums[1]), jnp.where(first, sums[1], sums[0])
    return jnp.concatenate([low, high], axis=2)


def solution(mesh):
    placed = (
        P(("frag", "space", "sub"), None, None),
        P(("frag", "space", "sub"), "aux", None, None),
        P(("frag", "space", "sub"), "aux"),
        P(("frag", "space", "sub"), "aux", None, None),
        P(("frag", "space", "sub"), "aux", None),
        P(("frag", "space", "aux"), "sub", None, None),
        P(("frag", "space", "aux"), "sub"),
    )
    return jax.shard_map(
        shards,
        mesh=mesh,
        in_specs=placed,
        out_specs=P(("frag", "space", "sub"), "aux", None),
        check_vma=False,
    )
```

```python
import functools

import jax
import jax.numpy as jnp
from jax import lax
from jax.experimental import pallas as pl
from jax.experimental.pallas import tpu as pltpu
from jax.sharding import PartitionSpec as P

BF16 = jnp.bfloat16
F32 = jnp.float32
NT = (((1,), (1,)), ((), ()))
VMEM_LIMIT = 32 * 1024 * 1024
VMEM = pl.BlockSpec(memory_space=pltpu.VMEM)
SMEM = pl.BlockSpec(memory_space=pltpu.SMEM)
ANY = pl.BlockSpec(memory_space=pl.ANY)


def fit_other_kernel(
    owned, half, groups, tile_hbm, domain_hbm, number_hbm, d_hbm, t_hbm, send_ref, slot_any, own_ref, t_ref,
    acc, tile_ref, domain_ref, number_ref, slot_ref, d_ref, small_sem, d_sem, t_sem,
):
    me = lax.axis_index("space")
    mine = lax.axis_index("sub")
    blocks, listed = t_ref.shape[:2]
    small = [
        pltpu.make_async_copy(tile_hbm, tile_ref, small_sem.at[0]),
        pltpu.make_async_copy(domain_hbm, domain_ref, small_sem.at[1]),
        pltpu.make_async_copy(number_hbm, number_ref, small_sem.at[2]),
    ]
    for copy in small:
        copy.start()
    copies, begin = [], 0
    for i, size in enumerate(groups):
        part = pl.ds(begin, size)
        copies.append(
            (
                pltpu.make_async_copy(d_hbm.at[part], d_ref.at[part], d_sem.at[i]),
                pltpu.make_async_copy(t_hbm.at[part], t_ref.at[part], t_sem.at[i]),
            )
        )
        begin += size
    for pair in copies:
        for copy in pair:
            copy.start()
    acc[...] = jnp.zeros_like(acc)
    for copy in small:
        copy.wait()
    other = pl.multiple_of((1 - mine) * half, half)
    own = pl.multiple_of(mine * half, half)
    begin = 0
    for size, pair in zip(groups, copies):
        for copy in pair:
            copy.wait()
        for p in range(begin, begin + size):
            rows = jnp.transpose(d_ref[p, :, pl.ds(other, half)])
            own_ref[p] = jnp.transpose(d_ref[p, :, pl.ds(own, half)])
            for k in range(listed):
                touched = tile_ref[p, k]
                slot = jnp.bitwise_xor(domain_ref[touched], me) * owned + number_ref[touched]
                slot_ref[p, k] = slot
                acc[slot] += jnp.dot(rows, t_ref[p, k], preferred_element_type=F32)
        begin += size
    slot_copy = pltpu.make_async_copy(slot_ref, slot_any, small_sem.at[3])
    slot_copy.start()
    send_ref[...] = acc[...].astype(BF16)
    slot_copy.wait()


def fit_other(block_tile, domain, number, densities, three_centre, domains, owned):
    blocks, listed, width, _ = three_centre.shape
    half = densities.shape[2] // 2
    count = domains * owned
    groups = (blocks // 4, 3 * blocks // 8, blocks - blocks // 4 - 3 * blocks // 8)
    operands = (block_tile, domain, number, densities, three_centre)
    operands = [pltpu.with_memory_space_constraint(operand, pltpu.HBM) for operand in operands]
    return pl.pallas_call(
        functools.partial(fit_other_kernel, owned, half, groups),
        in_specs=[pl.BlockSpec(memory_space=pltpu.HBM)] * 5,
        out_specs=[VMEM, ANY, VMEM, VMEM],
        scratch_shapes=[
            pltpu.VMEM((count, half, width), F32),
            pltpu.SMEM(block_tile.shape, jnp.int32),
            pltpu.SMEM(domain.shape, jnp.int32),
            pltpu.SMEM(number.shape, jnp.int32),
            pltpu.SMEM(block_tile.shape, jnp.int32),
            pltpu.VMEM(densities.shape, BF16),
            pltpu.SemaphoreType.DMA((4,)),
            pltpu.SemaphoreType.DMA((len(groups),)),
            pltpu.SemaphoreType.DMA((len(groups),)),
        ],
        out_shape=[
            jax.ShapeDtypeStruct((count, half, width), BF16),
            jax.ShapeDtypeStruct(block_tile.shape, jnp.int32),
            jax.ShapeDtypeStruct((blocks, half, width), BF16),
            jax.ShapeDtypeStruct(three_centre.shape, BF16),
        ],
        compiler_params=pltpu.CompilerParams(vmem_limit_bytes=VMEM_LIMIT),
        cost_estimate=pl.CostEstimate(
            flops=2 * blocks * listed * width * width * half,
            bytes_accessed=2 * (three_centre.size + densities.size),
            transcendentals=0,
        ),
        name="fit_other",
    )(*operands)


def fit_own_kernel(slot_any, own_ref, t_ref, keep_ref, acc, slot_ref, sem):
    slot_copy = pltpu.make_async_copy(slot_any, slot_ref, sem)
    slot_copy.start()
    acc[...] = jnp.zeros_like(acc)
    slot_copy.wait()
    for p in range(t_ref.shape[0]):
        rows = own_ref[p]
        for k in range(t_ref.shape[1]):
            acc[slot_ref[p, k]] += jnp.dot(rows, t_ref[p, k], preferred_element_type=F32)
    keep_ref[...] = acc[...].astype(BF16)


def fit_own(slots, own_rows, three_centre, count):
    blocks, listed, width, _ = three_centre.shape
    half = own_rows.shape[1]
    return pl.pallas_call(
        fit_own_kernel,
        in_specs=[ANY, VMEM, VMEM],
        out_specs=VMEM,
        scratch_shapes=[
            pltpu.VMEM((count, half, width), F32),
            pltpu.SMEM(slots.shape, jnp.int32),
            pltpu.SemaphoreType.DMA,
        ],
        out_shape=jax.ShapeDtypeStruct((count, half, width), BF16),
        compiler_params=pltpu.CompilerParams(vmem_limit_bytes=VMEM_LIMIT),
        cost_estimate=pl.CostEstimate(
            flops=2 * blocks * listed * width * width * half,
            bytes_accessed=2 * (three_centre.size + own_rows.size),
            transcendentals=0,
        ),
        name="fit_own",
    )(slots, own_rows, three_centre)


def metric_kernel(owned, count, mine_cols, peer_cols, near_ref, odd_ref, even_ref, m_ref, pm_ref, out_ref, window):
    me = lax.axis_index("space")
    aux = lax.axis_index("aux")
    own = owned * count
    window[:own] = near_ref[...]
    window[own : 2 * own] = even_ref[...]
    window[2 * own :] = odd_ref[...]

    def place(column):
        zone = column // own
        rest = column % own
        side = jnp.where((zone == 2) == (me % 2 == 0), 1, 2)
        block = jnp.where(zone == 1, 0, side)
        turned = (rest // owned + count - aux) % count
        return block * own + turned * owned + rest % owned

    for q in range(m_ref.shape[0]):
        picked, blocks = [], []
        for cols, mat in ((mine_cols, m_ref), (peer_cols, pm_ref)):
            for m in range(mat.shape[1]):
                picked.append(window[place(cols[q, m])])
                blocks.append(mat[q, m])
        out_ref[q] = lax.dot_general(
            jnp.concatenate(picked, axis=1),
            jnp.concatenate(blocks, axis=1),
            NT,
            preferred_element_type=F32,
        ).astype(BF16)


def metric(mine_cols, peer_cols, near, odd, even, m, pm, count):
    owned, listed, width, _ = m.shape
    half = near.shape[1]
    return pl.pallas_call(
        functools.partial(metric_kernel, owned, count),
        in_specs=[SMEM] * 2 + [VMEM] * 5,
        out_specs=VMEM,
        out_shape=jax.ShapeDtypeStruct((owned, half, width), BF16),
        scratch_shapes=[pltpu.VMEM((3 * owned * count, half, width), BF16)],
        compiler_params=pltpu.CompilerParams(vmem_limit_bytes=VMEM_LIMIT),
        cost_estimate=pl.CostEstimate(
            flops=4 * owned * listed * width * width * half,
            bytes_accessed=4 * m.size + 6 * near.size,
            transcendentals=0,
        ),
        name="metric",
    )(mine_cols, peer_cols, near, odd, even, m, pm)


def build_kernel(parts, order, slot_ref, t_ref, *rest):
    piece_refs, (out_ref, table) = rest[:-2], rest[-2:]
    aux = lax.axis_index("aux")
    blocks, listed, width, _ = t_ref.shape
    owned = piece_refs[0].shape[0]
    rows = width // parts
    for k, piece in zip(order, piece_refs):
        table[k * owned : (k + 1) * owned] = piece[...]
    for p in range(blocks):
        left = [t_ref[p, k] for k in range(listed)]
        right = [table[slot_ref[p, k]] for k in range(listed)]
        total = lax.dot_general(
            jnp.concatenate(left, axis=1), jnp.concatenate(right, axis=1), NT, preferred_element_type=F32
        ).astype(BF16)
        for part in range(parts):
            out_ref[lax.rem(part + parts - aux, parts), p] = total[part * rows : (part + 1) * rows]


def build(slots, three_centre, pieces, order, parts, name):
    blocks, listed, width, _ = three_centre.shape
    owned, half, _ = pieces[0].shape
    return pl.pallas_call(
        functools.partial(build_kernel, parts, order),
        in_specs=[SMEM] + [VMEM] * (1 + len(pieces)),
        out_specs=VMEM,
        out_shape=jax.ShapeDtypeStruct((parts, blocks, width // parts, half), BF16),
        scratch_shapes=[pltpu.VMEM((len(pieces) * owned, half, width), BF16)],
        compiler_params=pltpu.CompilerParams(vmem_limit_bytes=VMEM_LIMIT),
        cost_estimate=pl.CostEstimate(
            flops=2 * blocks * listed * width * width * half,
            bytes_accessed=2 * (three_centre.size + blocks * width * half),
            transcendentals=0,
        ),
        name=name,
    )(slots, three_centre, *pieces)


def exchange(array, axis, distance):
    return lax.ppermute(array, axis, [(i, i ^ distance) for i in range(lax.axis_size(axis))])


def ahead_by(array, axis, distance):
    count = lax.axis_size(axis)
    return lax.ppermute(array, axis, [(i, (i + distance) % count) for i in range(count)])


def pairs_from(array, axis, first):
    swaps = []
    for low in range(first, lax.axis_size(axis) - 1, 2):
        swaps += [(low, low + 1), (low + 1, low)]
    return lax.ppermute(array, axis, swaps)


def shards(
    densities, three_centre, block_tile, owner_domain, owner_tile, metric_inverse, metric_columns
):
    domains = lax.axis_size("space")
    aux_count = lax.axis_size("aux")
    touched = owner_tile.shape[-1]
    owned, _, width, _ = metric_inverse.shape
    half = densities.shape[2] // 2
    domain = owner_domain.reshape(touched)
    number = owner_tile.reshape(touched)

    send, slots, own_rows, three_centre = fit_other(
        block_tile, domain, number, densities, three_centre, domains, owned
    )
    got = exchange(send, "sub", 1)
    keep = fit_own(slots, own_rows, three_centre, domains * owned)
    chip = (keep.astype(F32) + got.astype(F32)).astype(BF16).reshape(domains, owned, half, width)
    chip, own_metric, own_columns = lax.optimization_barrier((chip, metric_inverse, metric_columns))
    arrived = [exchange(chip[k], "space", k) for k in range(1, domains)]
    peer_metric = exchange(own_metric, "sub", 1)
    peer_columns = exchange(own_columns, "sub", 1)
    arrived, peer_metric, peer_columns = lax.optimization_barrier((arrived[::-1], peer_metric, peer_columns))
    arrived = arrived[::-1]
    total = chip[0].astype(F32)
    for piece in arrived[::-1]:
        total = total + piece.astype(F32)
    fitted = total.astype(BF16)

    near = jnp.concatenate(
        [fitted] + [ahead_by(fitted, "aux", aux_count - k) for k in range(1, aux_count)]
    )
    odd = pairs_from(near, "space", 1)
    even = pairs_from(near, "space", 0)
    coefficients = metric(
        metric_columns, peer_columns, near, odd, even, metric_inverse, peer_metric, aux_count
    )

    order = [0] + list(range(domains - 1, 0, -1))
    pieces = [coefficients] + [exchange(coefficients, "space", k) for k in order[1:]]
    other = [exchange(piece, "sub", 1) for piece in pieces]

    sums = []
    for name, tiles in (("build_own", pieces), ("build_other", other)):
        parts = build(slots, three_centre, tiles, order, aux_count, name)
        terms = [parts[0]] + [ahead_by(parts[k], "aux", k) for k in range(1, aux_count)]
        sums.append(sum(term.astype(F32) for term in terms).astype(BF16))
    first = lax.axis_index("sub") == 0
    low, high = jnp.where(first, sums[0], sums[1]), jnp.where(first, sums[1], sums[0])
    return jnp.concatenate([low, high], axis=2)


def solution(mesh):
    placed = (
        P(("frag", "space", "sub"), None, None),
        P(("frag", "space", "sub"), "aux", None, None),
        P(("frag", "space", "sub"), "aux"),
        P(("frag", "space", "sub"), "aux", None, None),
        P(("frag", "space", "sub"), "aux", None),
        P(("frag", "space", "aux"), "sub", None, None),
        P(("frag", "space", "aux"), "sub"),
    )
    return jax.shard_map(
        shards,
        mesh=mesh,
        in_specs=placed,
        out_specs=P(("frag", "space", "sub"), "aux", None),
        check_vma=False,
    )
```

```python
import functools

import jax
import jax.numpy as jnp
from jax import lax
from jax.experimental import pallas as pl
from jax.experimental.pallas import tpu as pltpu
from jax.sharding import PartitionSpec as P

BF16 = jnp.bfloat16
F32 = jnp.float32
NT = (((1,), (1,)), ((), ()))
VMEM_LIMIT = 32 * 1024 * 1024
VMEM = pl.BlockSpec(memory_space=pltpu.VMEM)
SMEM = pl.BlockSpec(memory_space=pltpu.SMEM)
ANY = pl.BlockSpec(memory_space=pl.ANY)


def fit_other_kernel(
    owned, half, groups, tile_hbm, domain_hbm, number_hbm, d_hbm, t_hbm, send_ref, slot_any, own_ref, t_ref,
    acc, tile_ref, domain_ref, number_ref, slot_ref, d_ref, small_sem, d_sem, t_sem,
):
    me = lax.axis_index("space")
    mine = lax.axis_index("sub")
    blocks, listed = t_ref.shape[:2]
    small = [
        pltpu.make_async_copy(tile_hbm, tile_ref, small_sem.at[0]),
        pltpu.make_async_copy(domain_hbm, domain_ref, small_sem.at[1]),
        pltpu.make_async_copy(number_hbm, number_ref, small_sem.at[2]),
    ]
    for copy in small:
        copy.start()
    copies, begin = [], 0
    for i, size in enumerate(groups):
        part = pl.ds(begin, size)
        copies.append(
            (
                pltpu.make_async_copy(d_hbm.at[part], d_ref.at[part], d_sem.at[i]),
                pltpu.make_async_copy(t_hbm.at[part], t_ref.at[part], t_sem.at[i]),
            )
        )
        begin += size
    for pair in copies:
        for copy in pair:
            copy.start()
    acc[...] = jnp.zeros_like(acc)
    for copy in small:
        copy.wait()
    other = pl.multiple_of((1 - mine) * half, half)
    own = pl.multiple_of(mine * half, half)
    begin = 0
    for size, pair in zip(groups, copies):
        for copy in pair:
            copy.wait()
        for p in range(begin, begin + size):
            rows = jnp.transpose(d_ref[p, :, pl.ds(other, half)])
            own_ref[p] = jnp.transpose(d_ref[p, :, pl.ds(own, half)])
            for k in range(listed):
                touched = tile_ref[p, k]
                slot = jnp.bitwise_xor(domain_ref[touched], me) * owned + number_ref[touched]
                slot_ref[p, k] = slot
                acc[slot] += jnp.dot(rows, t_ref[p, k], preferred_element_type=F32)
        begin += size
    slot_copy = pltpu.make_async_copy(slot_ref, slot_any, small_sem.at[3])
    slot_copy.start()
    send_ref[...] = acc[...].astype(BF16)
    slot_copy.wait()


def fit_other(block_tile, domain, number, densities, three_centre, domains, owned):
    blocks, listed, width, _ = three_centre.shape
    half = densities.shape[2] // 2
    count = domains * owned
    groups = (blocks // 4, 3 * blocks // 8, blocks - blocks // 4 - 3 * blocks // 8)
    operands = (block_tile, domain, number, densities, three_centre)
    operands = [pltpu.with_memory_space_constraint(operand, pltpu.HBM) for operand in operands]
    return pl.pallas_call(
        functools.partial(fit_other_kernel, owned, half, groups),
        in_specs=[pl.BlockSpec(memory_space=pltpu.HBM)] * 5,
        out_specs=[VMEM, ANY, VMEM, VMEM],
        scratch_shapes=[
            pltpu.VMEM((count, half, width), F32),
            pltpu.SMEM(block_tile.shape, jnp.int32),
            pltpu.SMEM(domain.shape, jnp.int32),
            pltpu.SMEM(number.shape, jnp.int32),
            pltpu.SMEM(block_tile.shape, jnp.int32),
            pltpu.VMEM(densities.shape, BF16),
            pltpu.SemaphoreType.DMA((4,)),
            pltpu.SemaphoreType.DMA((len(groups),)),
            pltpu.SemaphoreType.DMA((len(groups),)),
        ],
        out_shape=[
            jax.ShapeDtypeStruct((count, half, width), BF16),
            jax.ShapeDtypeStruct(block_tile.shape, jnp.int32),
            jax.ShapeDtypeStruct((blocks, half, width), BF16),
            jax.ShapeDtypeStruct(three_centre.shape, BF16),
        ],
        compiler_params=pltpu.CompilerParams(vmem_limit_bytes=VMEM_LIMIT),
        cost_estimate=pl.CostEstimate(
            flops=2 * blocks * listed * width * width * half,
            bytes_accessed=2 * (three_centre.size + densities.size),
            transcendentals=0,
        ),
        name="fit_other",
    )(*operands)


def fit_own_kernel(slot_any, own_ref, t_ref, keep_ref, acc, slot_ref, sem):
    slot_copy = pltpu.make_async_copy(slot_any, slot_ref, sem)
    slot_copy.start()
    acc[...] = jnp.zeros_like(acc)
    slot_copy.wait()
    for p in range(t_ref.shape[0]):
        rows = own_ref[p]
        for k in range(t_ref.shape[1]):
            acc[slot_ref[p, k]] += jnp.dot(rows, t_ref[p, k], preferred_element_type=F32)
    keep_ref[...] = acc[...].astype(BF16)


def fit_own(slots, own_rows, three_centre, count):
    blocks, listed, width, _ = three_centre.shape
    half = own_rows.shape[1]
    return pl.pallas_call(
        fit_own_kernel,
        in_specs=[ANY, VMEM, VMEM],
        out_specs=VMEM,
        scratch_shapes=[
            pltpu.VMEM((count, half, width), F32),
            pltpu.SMEM(slots.shape, jnp.int32),
            pltpu.SemaphoreType.DMA,
        ],
        out_shape=jax.ShapeDtypeStruct((count, half, width), BF16),
        compiler_params=pltpu.CompilerParams(vmem_limit_bytes=VMEM_LIMIT),
        cost_estimate=pl.CostEstimate(
            flops=2 * blocks * listed * width * width * half,
            bytes_accessed=2 * (three_centre.size + own_rows.size),
            transcendentals=0,
        ),
        name="fit_own",
    )(slots, own_rows, three_centre)


def metric_kernel(owned, count, mine_cols, peer_cols, near_ref, *rest):
    odd_refs, even_refs, (m_ref, pm_ref, out_ref, window) = rest[:2], rest[2:-4], rest[-4:]
    me = lax.axis_index("space")
    aux = lax.axis_index("aux")
    own = owned * count
    window[:own] = near_ref[...]
    for begin, refs in ((own, even_refs), (2 * own, odd_refs)):
        for ref in refs:
            window[begin : begin + ref.shape[0]] = ref[...]
            begin += ref.shape[0]

    def place(column):
        zone = column // own
        rest = column % own
        side = jnp.where((zone == 2) == (me % 2 == 0), 1, 2)
        block = jnp.where(zone == 1, 0, side)
        turned = (rest // owned + count - aux) % count
        return block * own + turned * owned + rest % owned

    for q in range(m_ref.shape[0]):
        picked, blocks = [], []
        for cols, mat in ((mine_cols, m_ref), (peer_cols, pm_ref)):
            for m in range(mat.shape[1]):
                picked.append(window[place(cols[q, m])])
                blocks.append(mat[q, m])
        out_ref[q] = lax.dot_general(
            jnp.concatenate(picked, axis=1),
            jnp.concatenate(blocks, axis=1),
            NT,
            preferred_element_type=F32,
        ).astype(BF16)


def metric(mine_cols, peer_cols, near, odd, even, m, pm, count):
    owned, listed, width, _ = m.shape
    half = near.shape[1]
    return pl.pallas_call(
        functools.partial(metric_kernel, owned, count),
        in_specs=[SMEM] * 2 + [VMEM] * (3 + len(odd) + len(even)),
        out_specs=VMEM,
        out_shape=jax.ShapeDtypeStruct((owned, half, width), BF16),
        scratch_shapes=[pltpu.VMEM((3 * owned * count, half, width), BF16)],
        compiler_params=pltpu.CompilerParams(vmem_limit_bytes=VMEM_LIMIT),
        cost_estimate=pl.CostEstimate(
            flops=4 * owned * listed * width * width * half,
            bytes_accessed=4 * m.size + 6 * near.size,
            transcendentals=0,
        ),
        name="metric",
    )(mine_cols, peer_cols, near, *odd, *even, m, pm)


def build_kernel(parts, order, slot_ref, t_ref, *rest):
    piece_refs, (out_ref, table) = rest[:-2], rest[-2:]
    aux = lax.axis_index("aux")
    blocks, listed, width, _ = t_ref.shape
    owned = piece_refs[0].shape[0]
    rows = width // parts
    for k, piece in zip(order, piece_refs):
        table[k * owned : (k + 1) * owned] = piece[...]
    for p in range(blocks):
        left = [t_ref[p, k] for k in range(listed)]
        right = [table[slot_ref[p, k]] for k in range(listed)]
        total = lax.dot_general(
            jnp.concatenate(left, axis=1), jnp.concatenate(right, axis=1), NT, preferred_element_type=F32
        ).astype(BF16)
        for part in range(parts):
            out_ref[lax.rem(part + parts - aux, parts), p] = total[part * rows : (part + 1) * rows]


def build(slots, three_centre, pieces, order, parts, name):
    blocks, listed, width, _ = three_centre.shape
    owned, half, _ = pieces[0].shape
    return pl.pallas_call(
        functools.partial(build_kernel, parts, order),
        in_specs=[SMEM] + [VMEM] * (1 + len(pieces)),
        out_specs=VMEM,
        out_shape=jax.ShapeDtypeStruct((parts, blocks, width // parts, half), BF16),
        scratch_shapes=[pltpu.VMEM((len(pieces) * owned, half, width), BF16)],
        compiler_params=pltpu.CompilerParams(vmem_limit_bytes=VMEM_LIMIT),
        cost_estimate=pl.CostEstimate(
            flops=2 * blocks * listed * width * width * half,
            bytes_accessed=2 * (three_centre.size + blocks * width * half),
            transcendentals=0,
        ),
        name=name,
    )(slots, three_centre, *pieces)


def exchange(array, axis, distance):
    return lax.ppermute(array, axis, [(i, i ^ distance) for i in range(lax.axis_size(axis))])


def ahead_by(array, axis, distance):
    count = lax.axis_size(axis)
    return lax.ppermute(array, axis, [(i, (i + distance) % count) for i in range(count)])


def pairs_from(array, axis, first):
    swaps = []
    for low in range(first, lax.axis_size(axis) - 1, 2):
        swaps += [(low, low + 1), (low + 1, low)]
    return lax.ppermute(array, axis, swaps)


def shards(
    densities, three_centre, block_tile, owner_domain, owner_tile, metric_inverse, metric_columns
):
    domains = lax.axis_size("space")
    aux_count = lax.axis_size("aux")
    touched = owner_tile.shape[-1]
    owned, _, width, _ = metric_inverse.shape
    half = densities.shape[2] // 2
    domain = owner_domain.reshape(touched)
    number = owner_tile.reshape(touched)

    send, slots, own_rows, three_centre = fit_other(
        block_tile, domain, number, densities, three_centre, domains, owned
    )
    got = exchange(send, "sub", 1)
    keep = fit_own(slots, own_rows, three_centre, domains * owned)
    chip = (keep.astype(F32) + got.astype(F32)).astype(BF16).reshape(domains, owned, half, width)
    chip, own_metric, own_columns = lax.optimization_barrier((chip, metric_inverse, metric_columns))
    arrived = [exchange(chip[k], "space", k) for k in range(1, domains)]
    peer_metric = exchange(own_metric, "sub", 1)
    peer_columns = exchange(own_columns, "sub", 1)
    arrived, peer_metric, peer_columns = lax.optimization_barrier((arrived[::-1], peer_metric, peer_columns))
    arrived = arrived[::-1]
    total = chip[0].astype(F32)
    for piece in arrived[::-1]:
        total = total + piece.astype(F32)
    fitted = total.astype(BF16)

    odd = [pairs_from(fitted, "space", 1)]
    even = [pairs_from(fitted, "space", 0)]
    rest = [ahead_by(fitted, "aux", aux_count - k) for k in range(1, aux_count)]
    rest = jnp.concatenate(rest) if aux_count > 2 else rest[0]
    odd.append(pairs_from(rest, "space", 1))
    even.append(pairs_from(rest, "space", 0))
    near = jnp.concatenate([fitted, rest])
    coefficients = metric(
        metric_columns, peer_columns, near, odd, even, metric_inverse, peer_metric, aux_count
    )

    order = [0] + list(range(domains - 1, 0, -1))
    pieces = [coefficients] + [exchange(coefficients, "space", k) for k in order[1:]]
    other = [exchange(piece, "sub", 1) for piece in pieces]

    sums = []
    for name, tiles in (("build_own", pieces), ("build_other", other)):
        parts = build(slots, three_centre, tiles, order, aux_count, name)
        terms = [parts[0]] + [ahead_by(parts[k], "aux", k) for k in range(1, aux_count)]
        sums.append(sum(term.astype(F32) for term in terms).astype(BF16))
    first = lax.axis_index("sub") == 0
    low, high = jnp.where(first, sums[0], sums[1]), jnp.where(first, sums[1], sums[0])
    return jnp.concatenate([low, high], axis=2)


def solution(mesh):
    placed = (
        P(("frag", "space", "sub"), None, None),
        P(("frag", "space", "sub"), "aux", None, None),
        P(("frag", "space", "sub"), "aux"),
        P(("frag", "space", "sub"), "aux", None, None),
        P(("frag", "space", "sub"), "aux", None),
        P(("frag", "space", "aux"), "sub", None, None),
        P(("frag", "space", "aux"), "sub"),
    )
    return jax.shard_map(
        shards,
        mesh=mesh,
        in_specs=placed,
        out_specs=P(("frag", "space", "sub"), "aux", None),
        check_vma=False,
    )
```
